32 devices in a mesh: groups: 2 (over y), leaf: 8 (over z, x), sub: 2 (over core).
Axes of the slice: x: 2, y: 2, z: 4, core: 2. Of those that a mesh axis runs over, the one named last changes fastest.
Arguments:
- points: float32 [131072, 32], P(('groups', 'leaf', 'sub')), parts along dimension 0
- rhs: float32 [131072, 16], P(('groups', 'leaf', 'sub')), parts along dimension 0, may hold values from -0.4 to 0.4
- leaf_interpolator: float32 [256, 128, 512], P(('groups', 'leaf', 'sub')), parts along dimension 0, may hold values from -0.25 to 0.25
- node_basis: float32 [32, 128, 1024], P(('groups', 'leaf', 'sub')), parts along dimension 0, may hold values from -0.1875 to 0.1875
- leaf_skeleton: int32 [256, 128], P(('groups', 'leaf', 'sub')), parts along dimension 0, may hold values from 0 to 511, as said below
- node_skeleton: int32 [32, 128], P(('groups', 'leaf', 'sub')), parts along dimension 0, may hold values from 0 to 1023, as said below
- near_list: int32 [256, 4], P(('groups', 'leaf', 'sub')), parts along dimension 0, may hold values from 0 to 127, as said below
- far_owner: int32 [256, 16, 1], P(('groups', 'leaf', 'sub')), parts along dimension 0, may hold values from 0 to 15; in each aligned block of 128 rows (0 to 127, 128 to 255, ..., all dimensions but the last counted through in order) at most 16 rows name the same one
- far_node: int32 [256, 16], P(('groups', 'leaf', 'sub')), parts along dimension 0, may hold values from 0 to 8
Outputs:
- product: float32 [131072, 16], P(('groups', 'leaf', 'sub')), parts along dimension 0
The draws below stay inside these ranges and needn't reach their ends.
There are 2 independent parts, one for each index of `groups`. The reference program is written for one: setup_inputs(seed, part) draws one part's arguments, and reference() takes and returns one part's arrays. A program takes and returns all parts, laid end to end along the dimension named above; each array names one. Nothing has to cross between parts.
Inputs may be any that keep to these rules, and one draw needn't show every extreme that they name: `near_list`: entry 0 of each row is the row's own leaf; every entry lies within 8 leaves of it, and entry 1 lies exactly 8 leaves away. `leaf_skeleton`: the offsets of one row are distinct. `node_skeleton`: the positions of one row are distinct. `far_owner`: among the far entries of the leaves of one device, no owner is named more than 16 times, and in every draw some device names some owner exactly 16 times.
All inputs are finite; a program needn't handle non-finite values.
Results may differ from the reference program's by a relative error of at most 0.000076.
Values sent between devices are 32-bit elements; how exact they have to be, the bound alone decides.
A program may use at most 128 MiB of HBM per device.

```python
import math
import jax
import jax.numpy as jnp
import numpy as np
from jax import lax

D = 32
LEAF = 512
S = 128
R = 16
NEAR = 4
FAR = 16
LEAVES_DEV = 8
DEVS = 16
LEAVES = 128
POINTS = 65536
NODES_DEV = 9
CAP = 16


def draw_points(key, part):
    key = jax.random.fold_in(key, 11)
    center_key, noise_key = jax.random.split(key)
    centers = 0.7 * jax.random.normal(center_key, (LEAVES, D), jnp.float32)
    noise = jax.random.normal(noise_key, (POINTS, D), jnp.float32)
    return jnp.repeat(centers, LEAF, axis=0) + noise


def draw_near_list(key, part):
    key = jax.random.fold_in(key, 23)
    leaf_ids = jnp.arange(LEAVES, dtype=jnp.int32)
    neighbour = jnp.where(leaf_ids + LEAVES_DEV < LEAVES, leaf_ids + LEAVES_DEV, leaf_ids - LEAVES_DEV)
    offsets = jax.random.randint(key, (LEAVES, NEAR - 2), -LEAVES_DEV, LEAVES_DEV + 1, jnp.int32)
    others = jnp.clip(leaf_ids[:, None] + offsets, 0, LEAVES - 1)
    return jnp.concatenate([leaf_ids[:, None], neighbour[:, None], others], 1).astype(jnp.int32)


def draw_leaf_skeleton(key, part):
    key = jax.random.fold_in(key, 37)
    keys = jax.random.split(key, LEAVES)
    return jax.vmap(lambda one_key: jax.random.permutation(one_key, LEAF)[:S])(keys).astype(jnp.int32)


def draw_node_skeleton(key, part):
    key = jax.random.fold_in(key, 41)
    keys = jax.random.split(key, DEVS)
    return jax.vmap(lambda one_key: jax.random.permutation(one_key, LEAVES_DEV * S)[:S])(keys).astype(jnp.int32)


def touch_ends(entries, own_key, smallest, largest):
    longest = entries.shape.index(max(entries.shape))
    spots = []
    for shift in (0, 1):
        where = [jax.random.randint(jax.random.fold_in(own_key, axis), (), 0, length) for axis, length in enumerate(entries.shape)]
        where[longest] = (where[longest] + shift) % entries.shape[longest]
        spots.append(tuple(where))
    return entries.at[spots[0]].set(smallest).at[spots[1]].set(largest)


def block_scale(key, extent, cuts, least, top_value):
    factor_of, own = 1.0, jax.random.fold_in(key, 6)
    for dim, shards_of in cuts:
        steps = jnp.exp(jax.random.uniform(jax.random.fold_in(own, dim), (shards_of,), jnp.float32, least / len(cuts), top_value / len(cuts)))
        factor_of = factor_of * jnp.repeat(steps, extent[dim] // shards_of).reshape([-1 if axis == dim else 1 for axis in range(len(extent))])
    return factor_of


def assign_block(stream_key, own, number, rows, number_of, top, most, lean):
    order = jax.random.permutation(stream_key, number_of)
    heavy_load, usual = portions_of(number_of, rows * top, most, lean, True), portions_of(number_of, rows * top, most, lean, False)
    places = jnp.arange(number_of)

    def named(lengths, rotation):
        used = int((lengths > 0).sum())
        fixed = max(1, used // 4)
        passed = fixed + (places - fixed + rotation * (used - fixed)) % max(1, number_of - fixed)
        return jnp.zeros((number_of,), jnp.int32).at[order[jnp.where(places < fixed, places, passed)]].set(jnp.asarray(lengths, jnp.int32))

    lengths = jnp.where(number % 4 == 0, named(heavy_load, number // 4), named(usual, number - number // 4 - 1))
    mixed = jax.random.permutation(jax.random.fold_in(own, 3), number_of)
    donor, taker = mixed[0:number_of // 2 * 2:2], mixed[1:number_of // 2 * 2:2]
    room = jnp.minimum(lengths[donor] - 1, most - lengths[taker]) // 2
    room = jnp.where((donor == order[0]) | (taker == order[0]) | (lengths[taker] == 0), 0, jnp.maximum(room, 0))
    passed = jax.random.randint(jax.random.fold_in(own, 4), (number_of // 2,), 0, 1 << 20) % (room + 1)
    lengths = lengths.at[donor].add(-passed).at[taker].add(passed)
    members = jnp.searchsorted(jnp.cumsum(lengths), jnp.arange(rows * top), side="right").astype(jnp.int32)
    grid = members.reshape(top, rows).T
    grid = grid[jax.random.permutation(jax.random.fold_in(own, 1), rows)]
    rotation = jax.random.randint(jax.random.fold_in(own, 2), (rows, 1), 0, top)
    return jnp.take_along_axis(grid, (jnp.arange(top)[None, :] + rotation) % top, axis=1)


def portions_of(amount, total, limit, slope, full):
    portions = [(1 << 20) // math.isqrt(grade ** slope) + 1 for grade in range(1, amount + 1)]
    largest = limit if full else min(limit, max(-(-total // amount), total * portions[0] // sum(portions)))
    least = 1 if total - largest >= amount - 1 else 0
    holding, surplus = [largest] + [least] * (amount - 1), total - largest - least * (amount - 1)
    while surplus > 0:
        candidates = [i for i in range(1, amount) if holding[i] < largest] or [i for i in range(1, amount) if holding[i] < limit]
        whole, left = sum([portions[i] for i in candidates]), surplus
        for i in candidates:
            more = min(limit - holding[i], max(1, left * portions[i] // whole), surplus)
            holding[i] = holding[i] + more
            surplus = surplus - more
    return np.array(holding)


def bell_draw(key, shape, spread, most, pieces=(), kind=jnp.bfloat16):
    entries = spread * jax.random.normal(key, shape, jnp.float32)
    if pieces:
        entries = entries * block_scale(key, shape, pieces, -0.22, 0.18)
    return jnp.clip(entries, -most, most).astype(kind)


def setup_inputs(seed: int = 0, part: int = 0) -> dict:
    splits = jax.random.split(jax.random.key(seed), 10)
    part_splits = jax.random.split(jax.random.fold_in(splits[9], part), 10)
    points = draw_points(jax.random.fold_in(jax.random.fold_in(splits[9], part), 71), part)
    rhs = bell_draw(part_splits[1], (POINTS, R), 0.05, 0.4, ((0, 16),), jnp.float32)
    leaf_interpolator = bell_draw(part_splits[2], (LEAVES, S, LEAF), LEAF ** -0.5, 0.25, ((0, 16),), jnp.float32)
    node_basis = bell_draw(part_splits[3], (DEVS, S, LEAVES_DEV * S), (LEAVES_DEV * S) ** -0.5, 0.1875, ((0, 16),), jnp.float32)
    leaf_skeleton = draw_leaf_skeleton(jax.random.fold_in(jax.random.fold_in(splits[9], part), 71), part)
    node_skeleton = draw_node_skeleton(jax.random.fold_in(jax.random.fold_in(splits[9], part), 71), part)
    near_list = draw_near_list(jax.random.fold_in(jax.random.fold_in(splits[9], part), 71), part)
    far_owner_keys = jax.random.split(jax.random.fold_in(part_splits[7], 1), LEAVES * FAR // (LEAVES_DEV * FAR))
    far_owner_turns = jax.random.permutation(jax.random.fold_in(part_splits[7], 3), LEAVES * FAR // (LEAVES_DEV * FAR))
    far_owner = jax.vmap(lambda own, number: assign_block(jax.random.fold_in(part_splits[7], 2), own, number, LEAVES_DEV * FAR, DEVS, 1, CAP, 2))(far_owner_keys, far_owner_turns).reshape((LEAVES, FAR, 1))
    far_node = touch_ends(jax.random.randint(part_splits[8], (LEAVES, FAR), 0, NODES_DEV), jax.random.fold_in(part_splits[8], 1), 0, NODES_DEV - 1).astype(jnp.int32)
    return dict(points=points, rhs=rhs, leaf_interpolator=leaf_interpolator, node_basis=node_basis, leaf_skeleton=leaf_skeleton, node_skeleton=node_skeleton, near_list=near_list, far_owner=far_owner, far_node=far_node)


def kernel_apply(target_points, sources, weights):
    top_level = lax.Precision.HIGHEST
    inner_products = jnp.dot(target_points, sources.T, precision=top_level, preferred_element_type=jnp.float32)
    target_norm = jnp.sum(target_points * target_points, 1)
    source_norm = jnp.sum(sources * sources, 1)
    exponent_scale = 0.5 / target_points.shape[1]
    kernel = jnp.exp((2.0 * inner_products - target_norm[:, None] - source_norm[None, :]) * exponent_scale)
    return jnp.dot(kernel, weights, precision=top_level, preferred_element_type=jnp.float32)


def reference(points, rhs, leaf_interpolator, node_basis, leaf_skeleton, node_skeleton, near_list, far_owner, far_node):
    top_level = lax.Precision.HIGHEST
    leaf_points_all = points.reshape(LEAVES, LEAF, D)
    leaf_right_sides = rhs.reshape(LEAVES, LEAF, R)
    skeleton_values = jnp.einsum('wdo,woq->wdq', leaf_interpolator, leaf_right_sides, precision=top_level)
    skel_points = jnp.take_along_axis(leaf_points_all, leaf_skeleton[:, :, None], axis=1)
    stack_values = skeleton_values.reshape(DEVS, LEAVES_DEV * S, R)
    stack_points = skel_points.reshape(DEVS, LEAVES_DEV * S, D)
    node_values = jnp.einsum('dst,dtr->dsr', node_basis, stack_values, precision=top_level)
    node_points = jnp.take_along_axis(stack_points, node_skeleton[:, :, None], axis=1)
    table_points = jnp.concatenate([skel_points.reshape(DEVS, LEAVES_DEV, S, D), node_points[:, None]], 1).reshape(DEVS * NODES_DEV, S, D)
    table_values = jnp.concatenate([skeleton_values.reshape(DEVS, LEAVES_DEV, S, R), node_values[:, None]], 1).reshape(DEVS * NODES_DEV, S, R)
    far_ids = (far_owner[:, :, 0] * NODES_DEV + far_node).astype(jnp.int32)

    def single_leaf(leaf_pair):
        target_points, near_ids, node_ids = leaf_pair
        sources = jnp.concatenate([leaf_points_all[near_ids].reshape(-1, D), table_points[node_ids].reshape(-1, D)], 0)
        weights = jnp.concatenate([leaf_right_sides[near_ids].reshape(-1, R), table_values[node_ids].reshape(-1, R)], 0)
        return kernel_apply(target_points, sources, weights)

    result = lax.map(single_leaf, (leaf_points_all, near_list, far_ids))
    return result.reshape(POINTS, R)
```

```python
import functools
import math

import jax
import jax.numpy as jnp
from jax import lax
from jax.experimental import pallas as pl
from jax.experimental.pallas import tpu as pltpu
from jax.sharding import PartitionSpec as P

F32 = jnp.float32
BF16 = jnp.bfloat16
DEPTH = 256
NT = (((1,), (1,)), ((), ()))


def split2(x):
    hi = x.astype(BF16)
    return hi, (x - hi.astype(F32)).astype(BF16)


def split3(x):
    hi = x.astype(BF16)
    rest = x - hi.astype(F32)
    mid = rest.astype(BF16)
    return hi, mid, (rest - mid.astype(F32)).astype(BF16)


def norm_rows(norm, first):
    n1, n2, n3 = (part.astype(F32) for part in split3(norm))
    row = lax.broadcasted_iota(jnp.int32, (16, norm.shape[1]), 0)
    at = 0 if first else 3
    parts = jnp.where(row == at, n1, jnp.where(row == at + 1, n2, n3))
    inside = (row >= at) & (row < at + 3)
    return jnp.where(inside, parts, jnp.where(row < 6, 1.0, 0.0)).astype(BF16)


def features(x, norm, target):
    x1, x2, x3 = split3(x)
    order = (x1, x1, x2, x2, x1, x3) if target else (x1, x2, x1, x2, x3, x1)
    used = 6 * x.shape[0] + 16
    tail = jnp.zeros((DEPTH - used, x.shape[1]), BF16)
    return jnp.concatenate(order + (norm_rows(norm, target), tail), 0)


def target_features(x):
    scale = math.log2(math.e) / x.shape[0]
    norm = jnp.sum(x * x, 0, keepdims=True) * (-0.5 * scale)
    return features(x * scale, norm, True).T


def source_features(y):
    scale = math.log2(math.e) / y.shape[0]
    norm = jnp.sum(y * y, 0, keepdims=True) * (-0.5 * scale)
    return features(y, norm, False)


def tile(a, src, dims):
    b = source_features(src[:dims])
    w1, w2 = split2(src[dims:])
    weights = jnp.concatenate([w1, w2], 0)
    total = None
    for start in range(0, src.shape[1], 256):
        cut = slice(start, start + 256)
        k = jnp.exp2(jnp.dot(a, b[:, cut], preferred_element_type=F32))
        hi, lo = split2(k)
        w = weights[:, cut]
        part = lax.dot_general(
            jnp.concatenate([hi, lo], 1), jnp.concatenate([w, w], 1), NT,
            preferred_element_type=F32,
        )
        total = part if total is None else total + part
    return total


def prep_kernel(points, rhs, interp, basis, leaf_skel, node_skel, src, table):
    leaves, skel, size = interp.shape
    dims = points.shape[1]
    all_values, all_points = [], []
    for l in range(leaves):
        rows = slice(l * size, (l + 1) * size)
        xt = points[rows, :].T
        r = rhs[rows, :]
        src[l, :dims, :] = xt
        src[l, dims:, :] = r.T
        picks = lax.broadcasted_iota(jnp.int32, (size, skel), 0) == leaf_skel[l : l + 1, :]
        stacked = jnp.concatenate(split3(xt), 0)
        got = jnp.dot(stacked, picks.astype(BF16), preferred_element_type=F32)
        pts = got[:dims] + got[dims : 2 * dims] + got[2 * dims :]
        values = narrow_dot(interp[l], r)
        table[l, :dims, :] = pts
        table[l, dims:, :] = values.T
        all_values.append(values)
        all_points.append(pts)
    stack_points = jnp.concatenate(all_points, 1)
    picks = lax.broadcasted_iota(jnp.int32, (leaves * skel, skel), 0) == node_skel[0:1, :]
    stacked = jnp.concatenate(split3(stack_points), 0)
    got = jnp.dot(stacked, picks.astype(BF16), preferred_element_type=F32)
    table[leaves, :dims, :] = got[:dims] + got[dims : 2 * dims] + got[2 * dims :]
    values = narrow_dot(basis[0], jnp.concatenate(all_values, 0))
    table[leaves, dims:, :] = values.T


def narrow_dot(m, r):
    cols = r.shape[1]
    hi, lo = split2(m)
    parts = jnp.concatenate(split2(r), 1)
    got = jnp.dot(
        jnp.concatenate([hi, lo], 1), jnp.concatenate([parts, parts], 0),
        preferred_element_type=F32,
    )
    return got[:, :cols] + got[:, cols:]


def apply_kernel(ids, own, *refs, dims, per_tile, has_base):
    out = refs[-1]
    srcs = refs[: -2 if has_base else -1]
    a = target_features(own[0, :dims, :])
    total = None
    for t in range(0, len(srcs), per_tile):
        group = [ref[0] for ref in srcs[t : t + per_tile]]
        src = group[0] if per_tile == 1 else jnp.concatenate(group, 1)
        part = tile(a, src, dims)
        total = part if total is None else total + part
    cols = out.shape[1]
    result = total[:, :cols] + total[:, cols:]
    if has_base:
        result = result + refs[-2][...]
    out[...] = result


def run_apply(ids, own, table, base, columns, name):
    leaves, width, size = own.shape
    count = ids.shape[1]
    n = table.shape[2]
    pick = lambda f: lambda l, ids: (ids[l, f], 0, 0)
    in_specs = [pl.BlockSpec((1, width, size), lambda l, ids: (l, 0, 0))]
    in_specs += [pl.BlockSpec((1, width, n), pick(f)) for f in range(count)]
    operands = [own] + [table] * count
    if base is not None:
        in_specs.append(pl.BlockSpec((size, columns), lambda l, ids: (l, 0)))
        operands.append(base)
    entries = leaves * size * count * n
    return pl.pallas_call(
        functools.partial(
            apply_kernel, dims=width - columns, per_tile=max(1, size // n), has_base=base is not None
        ),
        grid_spec=pltpu.PrefetchScalarGridSpec(
            num_scalar_prefetch=1,
            grid=(leaves,),
            in_specs=in_specs,
            out_specs=pl.BlockSpec((size, columns), lambda l, ids: (l, 0)),
        ),
        out_shape=jax.ShapeDtypeStruct((leaves * size, columns), F32),
        compiler_params=pltpu.CompilerParams(vmem_limit_bytes=48 * 1024 * 1024),
        cost_estimate=pl.CostEstimate(
            flops=entries * 2 * 3 * 256, bytes_accessed=leaves * count * n * width * 4,
            transcendentals=entries,
        ),
        name=name,
    )(ids, *operands)


def shifted(value, axes):
    peers = lax.axis_size(axes)
    up = [(i, i + 1) for i in range(peers - 1)]
    down = [(j, i) for i, j in up]
    return lax.ppermute(value, axes, up), lax.ppermute(value, axes, down)


def per_device(
    points, rhs, leaf_interpolator, node_basis, leaf_skeleton, node_skeleton, near_list,
    far_owner, far_node,
):
    axes = ("leaf", "sub")
    leaves, skel, size = leaf_interpolator.shape
    dims, columns = points.shape[1], rhs.shape[1]
    width = dims + columns
    vmem = pl.BlockSpec(memory_space=pltpu.VMEM)
    src, table = pl.pallas_call(
        prep_kernel,
        in_specs=[vmem] * 6,
        out_specs=[vmem] * 2,
        out_shape=[
            jax.ShapeDtypeStruct((leaves, width, size), F32),
            jax.ShapeDtypeStruct((leaves + 1, width, skel), F32),
        ],
        compiler_params=pltpu.CompilerParams(vmem_limit_bytes=48 * 1024 * 1024),
        name="prep",
    )(points, rhs, leaf_interpolator, node_basis, leaf_skeleton, node_skeleton)
    every = lax.all_gather(table, axes, axis=0, tiled=True)
    before, after = shifted(src, axes)
    extended = jnp.concatenate([before, src, after], 0)
    near_ids = near_list - (lax.axis_index(axes) - 1) * leaves
    far_ids = far_owner[:, :, 0] * (leaves + 1) + far_node
    near = run_apply(near_ids, src, extended, None, columns, "near")
    return run_apply(far_ids, src, every, near, columns, "far")


def solution(mesh):
    rows = ("groups", "leaf", "sub")
    two, three = P(rows, None), P(rows, None, None)
    in_specs = (two, two, three, three, two, two, two, three, two)
    return jax.shard_map(
        per_device, mesh=mesh, in_specs=in_specs, out_specs=two, check_vma=False
    )
```

```python
import functools
import math

import jax
import jax.numpy as jnp
from jax import lax
from jax.experimental import pallas as pl
from jax.experimental.pallas import tpu as pltpu
from jax.sharding import PartitionSpec as P

F32 = jnp.float32
BF16 = jnp.bfloat16
DEPTH = 256
NT = (((1,), (1,)), ((), ()))


def split2(x):
    hi = x.astype(BF16)
    return hi, (x - hi.astype(F32)).astype(BF16)


def split3(x):
    hi = x.astype(BF16)
    rest = x - hi.astype(F32)
    mid = rest.astype(BF16)
    return hi, mid, (rest - mid.astype(F32)).astype(BF16)


def norm_rows(norm, first):
    n1, n2, n3 = (part.astype(F32) for part in split3(norm))
    row = lax.broadcasted_iota(jnp.int32, (16, norm.shape[1]), 0)
    at = 0 if first else 3
    parts = jnp.where(row == at, n1, jnp.where(row == at + 1, n2, n3))
    inside = (row >= at) & (row < at + 3)
    return jnp.where(inside, parts, jnp.where(row < 6, 1.0, 0.0)).astype(BF16)


def features(x, norm, target):
    x1, x2, x3 = split3(x)
    order = (x1, x1, x2, x2, x1, x3) if target else (x1, x2, x1, x2, x3, x1)
    used = 6 * x.shape[0] + 16
    tail = jnp.zeros((DEPTH - used, x.shape[1]), BF16)
    return jnp.concatenate(order + (norm_rows(norm, target), tail), 0)


def target_features(x):
    scale = math.log2(math.e) / x.shape[0]
    norm = jnp.sum(x * x, 0, keepdims=True) * (-0.5 * scale)
    return features(x * scale, norm, True).T


def source_features(y):
    scale = math.log2(math.e) / y.shape[0]
    norm = jnp.sum(y * y, 0, keepdims=True) * (-0.5 * scale)
    return features(y, norm, False)


def tile(a, src, dims):
    b = source_features(src[:dims])
    w1, w2 = split2(src[dims:])
    weights = jnp.concatenate([w1, w2], 0)
    total = None
    for start in range(0, src.shape[1], 256):
        cut = slice(start, start + 256)
        k = jnp.exp2(jnp.dot(a, b[:, cut], preferred_element_type=F32))
        hi, lo = split2(k)
        w = weights[:, cut]
        part = lax.dot_general(
            jnp.concatenate([hi, lo], 1), jnp.concatenate([w, w], 1), NT,
            preferred_element_type=F32,
        )
        total = part if total is None else total + part
    return total


def values_t(rt, m):
    cols = rt.shape[0]
    parts = jnp.concatenate(split2(rt), 0)
    hi, lo = split2(m)
    got = lax.dot_general(
        jnp.concatenate([parts, parts], 1), jnp.concatenate([hi, lo], 1), NT,
        preferred_element_type=F32,
    )
    return got[:cols] + got[cols:]


def picked_columns(xt, row):
    dims, size = xt.shape
    picks = lax.broadcasted_iota(jnp.int32, (size, row.shape[1]), 0) == row
    stacked = jnp.concatenate(split3(xt), 0)
    got = jnp.dot(stacked, picks.astype(BF16), preferred_element_type=F32)
    return got[:dims] + got[dims : 2 * dims] + got[2 * dims :]


def whole_kernel(
    points, rhs, interp, basis, leaf_skel, node_skel, near_list, far_owner, far_node,
    out, near, table, a_all, acc, near_send, near_recv, right_send, left_send, pair_send, recv,
):
    leaves, skel, size = interp.shape
    dims, columns = points.shape[0], rhs.shape[0]
    ring = lax.axis_size("leaf")
    leaf, sub = lax.axis_index("leaf"), lax.axis_index("sub")
    flat = leaf * 2 + sub
    devices = ring * 2
    half = ring // 2
    other = ring - 1 - half

    def leaf_at(position):
        q = lax.rem(position + ring, ring)
        return jnp.where(q < half, 2 * q, 2 * (ring - 1 - q) + 1)

    here = jnp.where(leaf % 2 == 0, leaf // 2, ring - 1 - leaf // 2)
    right = {"leaf": leaf_at(here + 1), "sub": sub}
    left = {"leaf": leaf_at(here - 1), "sub": sub}
    pair = {"leaf": leaf, "sub": 1 - sub}
    up_flat, down_flat = lax.rem(flat + 1, devices), lax.rem(flat + devices - 1, devices)
    up = {"leaf": up_flat // 2, "sub": up_flat % 2}
    down = {"leaf": down_flat // 2, "sub": down_flat % 2}

    barrier = pltpu.get_barrier_semaphore()
    for peer in (right, left, pair, up, down):
        pl.semaphore_signal(barrier, inc=1, device_id=peer, device_id_type=pl.DeviceIdType.MESH)
    for l in range(leaves):
        cut = slice(l * size, (l + 1) * size)
        near[leaves + l, :dims, :] = points[:, cut]
        near[leaves + l, dims:, :] = rhs[:, cut]

    @pl.when(flat == 0)
    def _():
        near[0:leaves] = jnp.zeros((leaves,) + near.shape[1:], F32)

    @pl.when(flat == devices - 1)
    def _():
        near[2 * leaves : 3 * leaves] = jnp.zeros((leaves,) + near.shape[1:], F32)

    pl.semaphore_wait(barrier, 5)

    def near_copy(to, first, which):
        return pltpu.make_async_remote_copy(
            src_ref=near.at[pl.ds(leaves, leaves)], dst_ref=near.at[pl.ds(first, leaves)],
            send_sem=near_send.at[which], recv_sem=near_recv.at[which],
            device_id=to, device_id_type=pl.DeviceIdType.MESH,
        )

    to_up, to_down = near_copy(up, 0, 0), near_copy(down, 2 * leaves, 1)

    @pl.when(flat < devices - 1)
    def _():
        to_up.start()

    @pl.when(flat > 0)
    def _():
        to_down.start()

    def block_copy(position, core, to, send):
        slot = leaf_at(position) * 2 + core
        return pltpu.make_async_remote_copy(
            src_ref=table.at[slot], dst_ref=table.at[slot],
            send_sem=send, recv_sem=recv.at[slot],
            device_id=to, device_id_type=pl.DeviceIdType.MESH,
        )

    def to_right(s):
        return block_copy(here - s, sub, right, right_send.at[s])

    def to_left(s):
        return block_copy(here + s, sub, left, left_send.at[s])

    def to_pair(position):
        q = lax.rem(position + ring, ring)
        return block_copy(position, sub, pair, pair_send.at[q])

    all_values, all_points = [], []
    for l in range(leaves):
        cut = slice(l * size, (l + 1) * size)
        pts = picked_columns(points[:, cut], leaf_skel[l : l + 1, :])
        values = values_t(rhs[:, cut], interp[l])
        table[flat, l, :dims, :] = pts
        table[flat, l, dims:, :] = values
        all_values.append(values)
        all_points.append(pts)
    table[flat, leaves, :dims, :] = picked_columns(jnp.concatenate(all_points, 1), node_skel[0:1, :])
    table[flat, leaves, dims:, :] = values_t(jnp.concatenate(all_values, 1), basis[0])
    to_right(0).start()
    to_left(0).start()
    to_pair(here).start()

    def own_tile(l, carry):
        block = near[leaves + l]
        a_all[l] = target_features(block[:dims])
        acc[l] = tile(a_all[l], block, dims)
        return carry

    lax.fori_loop(0, leaves, own_tile, 0)

    @pl.when(flat < devices - 1)
    def _():
        to_up.wait_send()
        to_down.wait_recv()

    @pl.when(flat > 0)
    def _():
        to_down.wait_send()
        to_up.wait_recv()

    def ring_step(s, carry):
        block_copy(here - 1 - s, sub, right, right_send.at[s]).wait_recv()

        @pl.when(s + 1 < half)
        def _():
            to_right(s + 1).start()

        to_pair(here - 1 - s).start()

        @pl.when(s < other)
        def _():
            block_copy(here + 1 + s, sub, left, left_send.at[s]).wait_recv()

            @pl.when(s + 1 < other)
            def _():
                to_left(s + 1).start()

            to_pair(here + 1 + s).start()

        return carry

    def near_tiles(l, carry):
        a = a_all[l]
        total = acc[l]
        for n in range(1, near_list.shape[1]):
            place = near_list[l, n] - (flat - 1) * leaves
            block = near[jnp.clip(place, 0, 3 * leaves - 1)]
            total = total + tile(a, block, dims)
        acc[l] = total
        return lax.fori_loop(l * half // leaves, (l + 1) * half // leaves, ring_step, carry)

    lax.fori_loop(0, leaves, near_tiles, 0)

    def finish(q, carry):
        block_copy(q, 1 - sub, pair, pair_send.at[q]).wait_recv()
        block_copy(q, sub, pair, pair_send.at[q]).wait_send()
        return carry

    lax.fori_loop(0, ring, finish, 0)
    for s in range(half):
        to_right(s).wait_send()
    for s in range(other):
        to_left(s).wait_send()

    def far_tiles(l, carry):
        a = a_all[l]
        total = acc[l]
        per_tile = size // skel
        for f in range(0, far_node.shape[1], per_tile):
            group = [table[far_owner[l, i], far_node[l, i]] for i in range(f, f + per_tile)]
            total = total + tile(a, jnp.concatenate(group, 1), dims)
        out[l] = (total[:, :columns] + total[:, columns:]).T
        return carry

    lax.fori_loop(0, leaves, far_tiles, 0)


def per_device(
    points, rhs, leaf_interpolator, node_basis, leaf_skeleton, node_skeleton, near_list,
    far_owner, far_node,
):
    leaves, skel, size = leaf_interpolator.shape
    dims, columns = points.shape[1], rhs.shape[1]
    width = dims + columns
    ring = lax.axis_size("leaf")
    vmem = pl.BlockSpec(memory_space=pltpu.VMEM)
    smem = pl.BlockSpec(memory_space=pltpu.SMEM)
    entries = leaves * size * size * 8
    dma = pltpu.SemaphoreType.DMA
    out = pl.pallas_call(
        whole_kernel,
        in_specs=[vmem] * 6 + [smem] * 3,
        out_specs=vmem,
        out_shape=jax.ShapeDtypeStruct((leaves, columns, size), F32),
        scratch_shapes=[
            pltpu.VMEM((3 * leaves, width, size), F32),
            pltpu.VMEM((2 * ring, leaves + 1, width, skel), F32),
            pltpu.VMEM((leaves, size, DEPTH), BF16),
            pltpu.VMEM((leaves, size, 2 * columns), F32),
            dma((2,)), dma((2,)), dma((ring,)), dma((ring,)), dma((ring,)), dma((2 * ring,)),
        ],
        compiler_params=pltpu.CompilerParams(
            vmem_limit_bytes=56 * 1024 * 1024, collective_id=0, has_side_effects=True
        ),
        cost_estimate=pl.CostEstimate(
            flops=entries * 2 * 3 * 256, bytes_accessed=8 * 1024 * 1024, transcendentals=entries
        ),
        name="whole",
    )(
        points.T, rhs.T, leaf_interpolator, node_basis, leaf_skeleton, node_skeleton, near_list,
        far_owner[:, :, 0], far_node,
    )
    return out.transpose(0, 2, 1).reshape(leaves * size, columns)


def solution(mesh):
    rows = ("groups", "leaf", "sub")
    two, three = P(rows, None), P(rows, None, None)
    in_specs = (two, two, three, three, two, two, two, three, two)
    return jax.shard_map(
        per_device, mesh=mesh, in_specs=in_specs, out_specs=two, check_vma=False
    )
```

```python
import functools
import math

import jax
import jax.numpy as jnp
from jax import lax
from jax.experimental import pallas as pl
from jax.experimental.pallas import tpu as pltpu
from jax.sharding import PartitionSpec as P

F32 = jnp.float32
BF16 = jnp.bfloat16
DEPTH = 256
NT = (((1,), (1,)), ((), ()))


def split2(x):
    hi = x.astype(BF16)
    return hi, (x - hi.astype(F32)).astype(BF16)


def split3(x):
    hi = x.astype(BF16)
    rest = x - hi.astype(F32)
    mid = rest.astype(BF16)
    return hi, mid, (rest - mid.astype(F32)).astype(BF16)


def norm_rows(norm, first):
    n1, n2, n3 = (part.astype(F32) for part in split3(norm))
    row = lax.broadcasted_iota(jnp.int32, (16, norm.shape[1]), 0)
    at = 0 if first else 3
    parts = jnp.where(row == at, n1, jnp.where(row == at + 1, n2, n3))
    inside = (row >= at) & (row < at + 3)
    return jnp.where(inside, parts, jnp.where(row < 6, 1.0, 0.0)).astype(BF16)


def features(x, norm, target):
    x1, x2, x3 = split3(x)
    order = (x1, x1, x2, x2, x1, x3) if target else (x1, x2, x1, x2, x3, x1)
    used = 6 * x.shape[0] + 16
    tail = jnp.zeros((DEPTH - used, x.shape[1]), BF16)
    return jnp.concatenate(order + (norm_rows(norm, target), tail), 0)


def target_features(x):
    scale = math.log2(math.e) / x.shape[0]
    norm = jnp.sum(x * x, 0, keepdims=True) * (-0.5 * scale)
    return features(x * scale, norm, True)


def source_features(y):
    scale = math.log2(math.e) / y.shape[0]
    norm = jnp.sum(y * y, 0, keepdims=True) * (-0.5 * scale)
    return features(y, norm, False)


def tile(a, src, dims):
    b = source_features(src[:dims]).T
    weights = jnp.concatenate(split2(src[dims:]), 0)
    k = jnp.exp2(jnp.dot(b, a, preferred_element_type=F32))
    return jnp.dot(
        jnp.concatenate([weights, weights], 1), jnp.concatenate(split2(k), 0),
        preferred_element_type=F32,
    )


def values_t(rt, m):
    cols = rt.shape[0]
    parts = jnp.concatenate(split2(rt), 0)
    hi, lo = split2(m)
    got = lax.dot_general(
        jnp.concatenate([parts, parts], 1), jnp.concatenate([hi, lo], 1), NT,
        preferred_element_type=F32,
    )
    return got[:cols] + got[cols:]


def picked_columns(xt, row):
    dims, size = xt.shape
    picks = lax.broadcasted_iota(jnp.int32, (size, row.shape[1]), 0) == row
    stacked = jnp.concatenate(split3(xt), 0)
    got = jnp.dot(stacked, picks.astype(BF16), preferred_element_type=F32)
    return got[:dims] + got[dims : 2 * dims] + got[2 * dims :]


def whole_kernel(
    points, rhs, interp, basis, leaf_skel, node_skel, near_list, far_owner, far_node,
    out, near, table, a_all, acc, near_send, near_recv, right_send, left_send, pair_send, recv,
):
    leaves, skel, size = interp.shape
    dims, columns = points.shape[0], rhs.shape[0]
    ring = lax.axis_size("leaf")
    leaf, sub = lax.axis_index("leaf"), lax.axis_index("sub")
    flat = leaf * 2 + sub
    devices = ring * 2
    half = ring // 2
    other = ring - 1 - half

    def leaf_at(position):
        q = lax.rem(position + ring, ring)
        return jnp.where(q < half, 2 * q, 2 * (ring - 1 - q) + 1)

    here = jnp.where(leaf % 2 == 0, leaf // 2, ring - 1 - leaf // 2)
    right = {"leaf": leaf_at(here + 1), "sub": sub}
    left = {"leaf": leaf_at(here - 1), "sub": sub}
    pair = {"leaf": leaf, "sub": 1 - sub}
    up_flat, down_flat = lax.rem(flat + 1, devices), lax.rem(flat + devices - 1, devices)
    up = {"leaf": up_flat // 2, "sub": up_flat % 2}
    down = {"leaf": down_flat // 2, "sub": down_flat % 2}

    barrier = pltpu.get_barrier_semaphore()
    for peer in (right, left, pair, up, down):
        pl.semaphore_signal(barrier, inc=1, device_id=peer, device_id_type=pl.DeviceIdType.MESH)
    for l in range(leaves):
        cut = slice(l * size, (l + 1) * size)
        near[leaves + l, :dims, :] = points[:, cut]
        near[leaves + l, dims:, :] = rhs[:, cut]

    @pl.when(flat == 0)
    def _():
        near[0:leaves] = jnp.zeros((leaves,) + near.shape[1:], F32)

    @pl.when(flat == devices - 1)
    def _():
        near[2 * leaves : 3 * leaves] = jnp.zeros((leaves,) + near.shape[1:], F32)

    pl.semaphore_wait(barrier, 5)

    def near_copy(to, first, which):
        return pltpu.make_async_remote_copy(
            src_ref=near.at[pl.ds(leaves, leaves)], dst_ref=near.at[pl.ds(first, leaves)],
            send_sem=near_send.at[which], recv_sem=near_recv.at[which],
            device_id=to, device_id_type=pl.DeviceIdType.MESH,
        )

    to_up, to_down = near_copy(up, 0, 0), near_copy(down, 2 * leaves, 1)

    @pl.when(flat < devices - 1)
    def _():
        to_up.start()

    @pl.when(flat > 0)
    def _():
        to_down.start()

    def block_copy(position, core, to, send):
        slot = leaf_at(position) * 2 + core
        return pltpu.make_async_remote_copy(
            src_ref=table.at[slot], dst_ref=table.at[slot],
            send_sem=send, recv_sem=recv.at[slot],
            device_id=to, device_id_type=pl.DeviceIdType.MESH,
        )

    def to_right(s):
        return block_copy(here - s, sub, right, right_send.at[s])

    def to_left(s):
        return block_copy(here + s, sub, left, left_send.at[s])

    def to_pair(position):
        q = lax.rem(position + ring, ring)
        return block_copy(position, sub, pair, pair_send.at[q])

    all_values, all_points = [], []
    for l in range(leaves):
        cut = slice(l * size, (l + 1) * size)
        pts = picked_columns(points[:, cut], leaf_skel[l : l + 1, :])
        values = values_t(rhs[:, cut], interp[l])
        table[flat, l, :dims, :] = pts
        table[flat, l, dims:, :] = values
        all_values.append(values)
        all_points.append(pts)
    table[flat, leaves, :dims, :] = picked_columns(jnp.concatenate(all_points, 1), node_skel[0:1, :])
    table[flat, leaves, dims:, :] = values_t(jnp.concatenate(all_values, 1), basis[0])
    to_right(0).start()
    to_left(0).start()
    to_pair(here).start()

    def own_tile(l, carry):
        block = near[leaves + l]
        a_all[l] = target_features(block[:dims])
        acc[l] = tile(a_all[l], block, dims)
        return carry

    lax.fori_loop(0, leaves, own_tile, 0)

    @pl.when(flat < devices - 1)
    def _():
        to_up.wait_send()
        to_down.wait_recv()

    @pl.when(flat > 0)
    def _():
        to_down.wait_send()
        to_up.wait_recv()

    def ring_step(s, carry):
        block_copy(here - 1 - s, sub, right, right_send.at[s]).wait_recv()

        @pl.when(s + 1 < half)
        def _():
            to_right(s + 1).start()

        to_pair(here - 1 - s).start()

        @pl.when(s < other)
        def _():
            block_copy(here + 1 + s, sub, left, left_send.at[s]).wait_recv()

            @pl.when(s + 1 < other)
            def _():
                to_left(s + 1).start()

            to_pair(here + 1 + s).start()

        return carry

    def near_tiles(l, carry):
        a = a_all[l]
        total = acc[l]
        for n in range(1, near_list.shape[0]):
            place = near_list[n, l] - (flat - 1) * leaves
            block = near[jnp.clip(place, 0, 3 * leaves - 1)]
            total = total + tile(a, block, dims)
        acc[l] = total
        return lax.fori_loop(l * half // leaves, (l + 1) * half // leaves, ring_step, carry)

    lax.fori_loop(0, leaves, near_tiles, 0)

    def finish(q, carry):
        block_copy(q, 1 - sub, pair, pair_send.at[q]).wait_recv()
        block_copy(q, sub, pair, pair_send.at[q]).wait_send()
        return carry

    lax.fori_loop(0, ring, finish, 0)
    for s in range(half):
        to_right(s).wait_send()
    for s in range(other):
        to_left(s).wait_send()

    def far_tiles(l, carry):
        a = a_all[l]
        total = acc[l]
        per_tile = size // skel
        for f in range(0, far_node.shape[1], per_tile):
            group = [table[far_owner[l, i], far_node[l, i]] for i in range(f, f + per_tile)]
            total = total + tile(a, jnp.concatenate(group, 1), dims)
        cut = pl.ds(pl.multiple_of(l * size, size), size)
        out[:, cut] = total[:columns] + total[columns:]
        return carry

    lax.fori_loop(0, leaves, far_tiles, 0)


def per_device(
    points, rhs, leaf_interpolator, node_basis, leaf_skeleton, node_skeleton, near_list,
    far_owner, far_node,
):
    leaves, skel, size = leaf_interpolator.shape
    dims, columns = points.shape[1], rhs.shape[1]
    width = dims + columns
    ring = lax.axis_size("leaf")
    vmem = pl.BlockSpec(memory_space=pltpu.VMEM)
    smem = pl.BlockSpec(memory_space=pltpu.SMEM)
    entries = leaves * size * size * 8
    dma = pltpu.SemaphoreType.DMA
    out = pl.pallas_call(
        whole_kernel,
        in_specs=[vmem] * 6 + [smem] * 3,
        out_specs=vmem,
        out_shape=jax.ShapeDtypeStruct((columns, leaves * size), F32),
        scratch_shapes=[
            pltpu.VMEM((3 * leaves, width, size), F32),
            pltpu.VMEM((2 * ring, leaves + 1, width, skel), F32),
            pltpu.VMEM((leaves, DEPTH, size), BF16),
            pltpu.VMEM((leaves, 2 * columns, size), F32),
            dma((2,)), dma((2,)), dma((ring,)), dma((ring,)), dma((ring,)), dma((2 * ring,)),
        ],
        compiler_params=pltpu.CompilerParams(
            vmem_limit_bytes=56 * 1024 * 1024, collective_id=0, has_side_effects=True
        ),
        cost_estimate=pl.CostEstimate(
            flops=entries * 2 * 3 * 256, bytes_accessed=8 * 1024 * 1024, transcendentals=entries
        ),
        name="whole",
    )(
        points.T, rhs.T, leaf_interpolator, node_basis, leaf_skeleton, node_skeleton, near_list.T,
        far_owner[:, :, 0], far_node,
    )
    return out.T


def solution(mesh):
    rows = ("groups", "leaf", "sub")
    two, three = P(rows, None), P(rows, None, None)
    in_specs = (two, two, three, three, two, two, two, three, two)
    return jax.shard_map(
        per_device, mesh=mesh, in_specs=in_specs, out_specs=two, check_vma=False
    )
```

```python
import functools
import math

import jax
import jax.numpy as jnp
from jax import lax
from jax.experimental import pallas as pl
from jax.experimental.pallas import tpu as pltpu
from jax.sharding import PartitionSpec as P

F32 = jnp.float32
BF16 = jnp.bfloat16
DEPTH = 256
NT = (((1,), (1,)), ((), ()))


def split2(x):
    hi = x.astype(BF16)
    return hi, (x - hi.astype(F32)).astype(BF16)


def split3(x):
    hi = x.astype(BF16)
    rest = x - hi.astype(F32)
    mid = rest.astype(BF16)
    return hi, mid, (rest - mid.astype(F32)).astype(BF16)


def norm_rows(norm, first):
    n1, n2, n3 = (part.astype(F32) for part in split3(norm))
    row = lax.broadcasted_iota(jnp.int32, (16, norm.shape[1]), 0)
    at = 0 if first else 3
    parts = jnp.where(row == at, n1, jnp.where(row == at + 1, n2, n3))
    inside = (row >= at) & (row < at + 3)
    return jnp.where(inside, parts, jnp.where(row < 6, 1.0, 0.0)).astype(BF16)


def features(x, norm, target):
    x1, x2, x3 = split3(x)
    order = (x1, x1, x2, x2, x1, x3) if target else (x1, x2, x1, x2, x3, x1)
    used = 6 * x.shape[0] + 16
    tail = jnp.zeros((DEPTH - used, x.shape[1]), BF16)
    return jnp.concatenate(order + (norm_rows(norm, target), tail), 0)


def target_features(x):
    scale = math.log2(math.e) / x.shape[0]
    norm = jnp.sum(x * x, 0, keepdims=True) * (-0.5 * scale)
    return features(x * scale, norm, True)


def source_features(y):
    scale = math.log2(math.e) / y.shape[0]
    norm = jnp.sum(y * y, 0, keepdims=True) * (-0.5 * scale)
    return features(y, norm, False)


def tile(a, src, dims):
    b = source_features(src[:dims]).T
    weights = jnp.concatenate(split2(src[dims:]), 0)
    k = jnp.exp2(jnp.dot(b, a, preferred_element_type=F32))
    return jnp.dot(
        jnp.concatenate([weights, weights], 1), jnp.concatenate(split2(k), 0),
        preferred_element_type=F32,
    )


def values_t(rt, m):
    cols = rt.shape[0]
    parts = jnp.concatenate(split2(rt), 0)
    hi, lo = split2(m)
    got = lax.dot_general(
        jnp.concatenate([parts, parts], 1), jnp.concatenate([hi, lo], 1), NT,
        preferred_element_type=F32,
    )
    return got[:cols] + got[cols:]


def picked_columns(xt, row):
    dims, size = xt.shape
    picks = lax.broadcasted_iota(jnp.int32, (size, row.shape[1]), 0) == row
    stacked = jnp.concatenate(split3(xt), 0)
    got = jnp.dot(stacked, picks.astype(BF16), preferred_element_type=F32)
    return got[:dims] + got[dims : 2 * dims] + got[2 * dims :]


def whole_kernel(
    points, rhs, interp, basis, leaf_skel, node_skel, near_list, far_owner, far_node,
    out, near, table, a_all, acc, near_send, near_recv, right_send, left_send, pair_send, recv,
):
    leaves, skel, size = interp.shape
    dims, columns = points.shape[0], rhs.shape[0]
    ring = lax.axis_size("leaf")
    leaf, sub = lax.axis_index("leaf"), lax.axis_index("sub")
    flat = leaf * 2 + sub
    devices = ring * 2
    half = ring // 2
    other = ring - 1 - half

    def leaf_at(position):
        q = lax.rem(position + ring, ring)
        return jnp.where(q < half, 2 * q, 2 * (ring - 1 - q) + 1)

    here = jnp.where(leaf % 2 == 0, leaf // 2, ring - 1 - leaf // 2)
    right = {"leaf": leaf_at(here + 1), "sub": sub}
    left = {"leaf": leaf_at(here - 1), "sub": sub}
    pair = {"leaf": leaf, "sub": 1 - sub}
    up_flat, down_flat = lax.rem(flat + 1, devices), lax.rem(flat + devices - 1, devices)
    up = {"leaf": up_flat // 2, "sub": up_flat % 2}
    down = {"leaf": down_flat // 2, "sub": down_flat % 2}

    barrier = pltpu.get_barrier_semaphore()
    for peer in (right, left, pair, up, down):
        pl.semaphore_signal(barrier, inc=1, device_id=peer, device_id_type=pl.DeviceIdType.MESH)
    for l in range(leaves):
        cut = slice(l * size, (l + 1) * size)
        near[leaves + l, :dims, :] = points[:, cut]
        near[leaves + l, dims:, :] = rhs[:, cut]

    @pl.when(flat == 0)
    def _():
        near[0:leaves] = jnp.zeros((leaves,) + near.shape[1:], F32)

    @pl.when(flat == devices - 1)
    def _():
        near[2 * leaves : 3 * leaves] = jnp.zeros((leaves,) + near.shape[1:], F32)

    pl.semaphore_wait(barrier, 5)

    def near_copy(to, first, which):
        return pltpu.make_async_remote_copy(
            src_ref=near.at[pl.ds(leaves, leaves)], dst_ref=near.at[pl.ds(first, leaves)],
            send_sem=near_send.at[which], recv_sem=near_recv.at[which],
            device_id=to, device_id_type=pl.DeviceIdType.MESH,
        )

    to_up, to_down = near_copy(up, 0, 0), near_copy(down, 2 * leaves, 1)

    def block_copy(position, core, to, send):
        slot = leaf_at(position) * 2 + core
        return pltpu.make_async_remote_copy(
            src_ref=table.at[slot], dst_ref=table.at[slot],
            send_sem=send, recv_sem=recv.at[slot],
            device_id=to, device_id_type=pl.DeviceIdType.MESH,
        )

    def to_right(s):
        return block_copy(here - s, sub, right, right_send.at[s])

    def to_left(s):
        return block_copy(here + s, sub, left, left_send.at[s])

    def to_pair(position):
        q = lax.rem(position + ring, ring)
        return block_copy(position, sub, pair, pair_send.at[q])

    all_values, all_points = [], []
    for l in range(leaves):
        cut = slice(l * size, (l + 1) * size)
        pts = picked_columns(points[:, cut], leaf_skel[l : l + 1, :])
        values = values_t(rhs[:, cut], interp[l])
        table[flat, l, :dims, :] = pts
        table[flat, l, dims:, :] = values
        all_values.append(values)
        all_points.append(pts)
    table[flat, leaves, :dims, :] = picked_columns(jnp.concatenate(all_points, 1), node_skel[0:1, :])
    table[flat, leaves, dims:, :] = values_t(jnp.concatenate(all_values, 1), basis[0])
    to_right(0).start()
    to_left(0).start()
    to_pair(here).start()

    def own_tile(l, carry):
        block = near[leaves + l]
        a_all[l] = target_features(block[:dims])
        acc[l] = tile(a_all[l], block, dims)
        return carry

    lax.fori_loop(0, leaves, own_tile, 0)

    def ring_step(s, carry):
        block_copy(here - 1 - s, sub, right, right_send.at[s]).wait_recv()

        @pl.when(s + 1 < half)
        def _():
            to_right(s + 1).start()

        to_pair(here - 1 - s).start()

        @pl.when(s < other)
        def _():
            block_copy(here + 1 + s, sub, left, left_send.at[s]).wait_recv()

            @pl.when(s + 1 < other)
            def _():
                to_left(s + 1).start()

            to_pair(here + 1 + s).start()

        return carry

    early = min(3, half)
    lax.fori_loop(0, early, ring_step, 0)

    @pl.when(flat < devices - 1)
    def _():
        to_up.start()

    @pl.when(flat > 0)
    def _():
        to_down.start()

    lax.fori_loop(early, half, ring_step, 0)

    def finish(q, carry):
        block_copy(q, 1 - sub, pair, pair_send.at[q]).wait_recv()
        block_copy(q, sub, pair, pair_send.at[q]).wait_send()
        return carry

    lax.fori_loop(0, ring, finish, 0)
    for s in range(half):
        to_right(s).wait_send()
    for s in range(other):
        to_left(s).wait_send()

    def far_tiles(l, carry):
        a = a_all[l]
        total = acc[l]
        per_tile = size // skel
        for f in range(0, far_node.shape[1], per_tile):
            group = [table[far_owner[l, i], far_node[l, i]] for i in range(f, f + per_tile)]
            total = total + tile(a, jnp.concatenate(group, 1), dims)
        acc[l] = total
        return carry

    lax.fori_loop(0, leaves, far_tiles, 0)

    @pl.when(flat < devices - 1)
    def _():
        to_up.wait_send()
        to_down.wait_recv()

    @pl.when(flat > 0)
    def _():
        to_down.wait_send()
        to_up.wait_recv()

    def near_tiles(l, carry):
        a = a_all[l]
        total = acc[l]
        for n in range(1, near_list.shape[0]):
            place = near_list[n, l] - (flat - 1) * leaves
            block = near[jnp.clip(place, 0, 3 * leaves - 1)]
            total = total + tile(a, block, dims)
        cut = pl.ds(pl.multiple_of(l * size, size), size)
        out[:, cut] = total[:columns] + total[columns:]
        return carry

    lax.fori_loop(0, leaves, near_tiles, 0)


def per_device(
    points, rhs, leaf_interpolator, node_basis, leaf_skeleton, node_skeleton, near_list,
    far_owner, far_node,
):
    leaves, skel, size = leaf_interpolator.shape
    dims, columns = points.shape[1], rhs.shape[1]
    width = dims + columns
    ring = lax.axis_size("leaf")
    vmem = pl.BlockSpec(memory_space=pltpu.VMEM)
    smem = pl.BlockSpec(memory_space=pltpu.SMEM)
    entries = leaves * size * size * 8
    dma = pltpu.SemaphoreType.DMA
    out = pl.pallas_call(
        whole_kernel,
        in_specs=[vmem] * 6 + [smem] * 3,
        out_specs=vmem,
        out_shape=jax.ShapeDtypeStruct((columns, leaves * size), F32),
        scratch_shapes=[
            pltpu.VMEM((3 * leaves, width, size), F32),
            pltpu.VMEM((2 * ring, leaves + 1, width, skel), F32),
            pltpu.VMEM((leaves, DEPTH, size), BF16),
            pltpu.VMEM((leaves, 2 * columns, size), F32),
            dma((2,)), dma((2,)), dma((ring,)), dma((ring,)), dma((ring,)), dma((2 * ring,)),
        ],
        compiler_params=pltpu.CompilerParams(
            vmem_limit_bytes=56 * 1024 * 1024, collective_id=0, has_side_effects=True
        ),
        cost_estimate=pl.CostEstimate(
            flops=entries * 2 * 3 * 256, bytes_accessed=8 * 1024 * 1024, transcendentals=entries
        ),
        name="whole",
    )(
        points.T, rhs.T, leaf_interpolator, node_basis, leaf_skeleton, node_skeleton, near_list.T,
        far_owner[:, :, 0], far_node,
    )
    return out.T


def solution(mesh):
    rows = ("groups", "leaf", "sub")
    two, three = P(rows, None), P(rows, None, None)
    in_specs = (two, two, three, three, two, two, two, three, two)
    return jax.shard_map(
        per_device, mesh=mesh, in_specs=in_specs, out_specs=two, check_vma=False
    )
```

```python
import functools
import math

import jax
import jax.numpy as jnp
from jax import lax
from jax.experimental import pallas as pl
from jax.experimental.pallas import tpu as pltpu
from jax.sharding import PartitionSpec as P

F32 = jnp.float32
BF16 = jnp.bfloat16
DEPTH = 256
NT = (((1,), (1,)), ((), ()))


def split2(x):
    hi = x.astype(BF16)
    return hi, (x - hi.astype(F32)).astype(BF16)


def split3(x):
    hi = x.astype(BF16)
    rest = x - hi.astype(F32)
    mid = rest.astype(BF16)
    return hi, mid, (rest - mid.astype(F32)).astype(BF16)


def norm_rows(norm, first):
    n1, n2, n3 = (part.astype(F32) for part in split3(norm))
    row = lax.broadcasted_iota(jnp.int32, (16, norm.shape[1]), 0)
    at = 0 if first else 3
    parts = jnp.where(row == at, n1, jnp.where(row == at + 1, n2, n3))
    inside = (row >= at) & (row < at + 3)
    return jnp.where(inside, parts, jnp.where(row < 6, 1.0, 0.0)).astype(BF16)


def features(x, norm, target):
    x1, x2, x3 = split3(x)
    order = (x1, x1, x2, x2, x1, x3) if target else (x1, x2, x1, x2, x3, x1)
    used = 6 * x.shape[0] + 16
    tail = jnp.zeros((DEPTH - used, x.shape[1]), BF16)
    return jnp.concatenate(order + (norm_rows(norm, target), tail), 0)


def target_features(x):
    scale = math.log2(math.e) / x.shape[0]
    norm = jnp.sum(x * x, 0, keepdims=True) * (-0.5 * scale)
    return features(x * scale, norm, True)


def source_features(y):
    scale = math.log2(math.e) / y.shape[0]
    norm = jnp.sum(y * y, 0, keepdims=True) * (-0.5 * scale)
    return features(y, norm, False)


def tile(a, src, dims):
    b = source_features(src[:dims]).T
    weights = jnp.concatenate(split2(src[dims:]), 0)
    k = jnp.exp2(jnp.dot(b, a, preferred_element_type=F32))
    return jnp.dot(
        jnp.concatenate([weights, weights], 1), jnp.concatenate(split2(k), 0),
        preferred_element_type=F32,
    )


def values_t(rt, m):
    cols = rt.shape[0]
    parts = jnp.concatenate(split2(rt), 0)
    hi, lo = split2(m)
    got = lax.dot_general(
        jnp.concatenate([parts, parts], 1), jnp.concatenate([hi, lo], 1), NT,
        preferred_element_type=F32,
    )
    return got[:cols] + got[cols:]


def picked_columns(xt, row):
    dims, size = xt.shape
    picks = lax.broadcasted_iota(jnp.int32, (size, row.shape[1]), 0) == row
    stacked = jnp.concatenate(split3(xt), 0)
    got = jnp.dot(stacked, picks.astype(BF16), preferred_element_type=F32)
    return got[:dims] + got[dims : 2 * dims] + got[2 * dims :]


def whole_kernel(
    points, rhs, interp, basis, leaf_skel, node_skel, near_list, far_owner, far_node,
    out, near, table, a_all, acc, near_send, near_recv, right_send, left_send, pair_send, recv,
):
    leaves, skel, size = interp.shape
    dims, columns = points.shape[0], rhs.shape[0]
    ring = lax.axis_size("leaf")
    leaf, sub = lax.axis_index("leaf"), lax.axis_index("sub")
    flat = leaf * 2 + sub
    devices = ring * 2
    half = ring // 2
    other = ring - 1 - half

    def leaf_at(position):
        q = lax.rem(position + ring, ring)
        return jnp.where(q < half, 2 * q, 2 * (ring - 1 - q) + 1)

    here = jnp.where(leaf % 2 == 0, leaf // 2, ring - 1 - leaf // 2)
    right = {"leaf": leaf_at(here + 1), "sub": sub}
    left = {"leaf": leaf_at(here - 1), "sub": sub}
    pair = {"leaf": leaf, "sub": 1 - sub}
    up_flat, down_flat = lax.rem(flat + 1, devices), lax.rem(flat + devices - 1, devices)
    up = {"leaf": up_flat // 2, "sub": up_flat % 2}
    down = {"leaf": down_flat // 2, "sub": down_flat % 2}

    barrier = pltpu.get_barrier_semaphore()
    for peer in (right, left, pair, up, down):
        pl.semaphore_signal(barrier, inc=1, device_id=peer, device_id_type=pl.DeviceIdType.MESH)
    for l in range(leaves):
        cut = slice(l * size, (l + 1) * size)
        near[leaves + l, :dims, :] = points[:, cut]
        near[leaves + l, dims:, :] = rhs[:, cut]

    @pl.when(flat == 0)
    def _():
        near[0:leaves] = jnp.zeros((leaves,) + near.shape[1:], F32)

    @pl.when(flat == devices - 1)
    def _():
        near[2 * leaves : 3 * leaves] = jnp.zeros((leaves,) + near.shape[1:], F32)

    pl.semaphore_wait(barrier, 5)

    def near_copy(to, first, which):
        return pltpu.make_async_remote_copy(
            src_ref=near.at[pl.ds(leaves, leaves)], dst_ref=near.at[pl.ds(first, leaves)],
            send_sem=near_send.at[which], recv_sem=near_recv.at[which],
            device_id=to, device_id_type=pl.DeviceIdType.MESH,
        )

    to_up, to_down = near_copy(up, 0, 0), near_copy(down, 2 * leaves, 1)

    def block_copy(position, core, to, send):
        slot = leaf_at(position) * 2 + core
        return pltpu.make_async_remote_copy(
            src_ref=table.at[slot], dst_ref=table.at[slot],
            send_sem=send, recv_sem=recv.at[slot],
            device_id=to, device_id_type=pl.DeviceIdType.MESH,
        )

    def to_right(s):
        return block_copy(here - s, sub, right, right_send.at[s])

    def to_left(s):
        return block_copy(here + s, sub, left, left_send.at[s])

    def to_pair(position):
        q = lax.rem(position + ring, ring)
        return block_copy(position, sub, pair, pair_send.at[q])

    all_values, all_points = [], []
    for l in range(leaves):
        cut = slice(l * size, (l + 1) * size)
        pts = picked_columns(points[:, cut], leaf_skel[l : l + 1, :])
        values = values_t(rhs[:, cut], interp[l])
        table[flat, l, :dims, :] = pts
        table[flat, l, dims:, :] = values
        all_values.append(values)
        all_points.append(pts)
    table[flat, leaves, :dims, :] = picked_columns(jnp.concatenate(all_points, 1), node_skel[0:1, :])
    table[flat, leaves, dims:, :] = values_t(jnp.concatenate(all_values, 1), basis[0])
    to_right(0).start()
    to_left(0).start()
    to_pair(here).start()

    def own_tile(l, carry):
        block = near[leaves + l]
        a_all[l] = target_features(block[:dims])
        acc[l] = tile(a_all[l], block, dims)
        return carry

    lax.fori_loop(0, leaves, own_tile, 0)

    def ring_step(s, carry):
        block_copy(here - 1 - s, sub, right, right_send.at[s]).wait_recv()

        @pl.when(s + 1 < half)
        def _():
            to_right(s + 1).start()

        to_pair(here - 1 - s).start()

        @pl.when(s < other)
        def _():
            block_copy(here + 1 + s, sub, left, left_send.at[s]).wait_recv()

            @pl.when(s + 1 < other)
            def _():
                to_left(s + 1).start()

            to_pair(here + 1 + s).start()

        return carry

    early = half
    lax.fori_loop(0, early, ring_step, 0)

    @pl.when(flat < devices - 1)
    def _():
        to_up.start()

    @pl.when(flat > 0)
    def _():
        to_down.start()

    lax.fori_loop(early, half, ring_step, 0)

    def finish(q, carry):
        block_copy(q, 1 - sub, pair, pair_send.at[q]).wait_recv()
        block_copy(q, sub, pair, pair_send.at[q]).wait_send()
        return carry

    lax.fori_loop(0, ring, finish, 0)
    for s in range(half):
        to_right(s).wait_send()
    for s in range(other):
        to_left(s).wait_send()

    def far_tiles(l, carry):
        a = a_all[l]
        total = acc[l]
        per_tile = size // skel
        for f in range(0, far_node.shape[1], per_tile):
            group = [table[far_owner[l, i], far_node[l, i]] for i in range(f, f + per_tile)]
            total = total + tile(a, jnp.concatenate(group, 1), dims)
        acc[l] = total
        return carry

    lax.fori_loop(0, leaves, far_tiles, 0)

    @pl.when(flat < devices - 1)
    def _():
        to_up.wait_send()
        to_down.wait_recv()

    @pl.when(flat > 0)
    def _():
        to_down.wait_send()
        to_up.wait_recv()

    def near_tiles(l, carry):
        a = a_all[l]
        total = acc[l]
        for n in range(1, near_list.shape[0]):
            place = near_list[n, l] - (flat - 1) * leaves
            block = near[jnp.clip(place, 0, 3 * leaves - 1)]
            total = total + tile(a, block, dims)
        cut = pl.ds(pl.multiple_of(l * size, size), size)
        out[:, cut] = total[:columns] + total[columns:]
        return carry

    lax.fori_loop(0, leaves, near_tiles, 0)


def per_device(
    points, rhs, leaf_interpolator, node_basis, leaf_skeleton, node_skeleton, near_list,
    far_owner, far_node,
):
    leaves, skel, size = leaf_interpolator.shape
    dims, columns = points.shape[1], rhs.shape[1]
    width = dims + columns
    ring = lax.axis_size("leaf")
    vmem = pl.BlockSpec(memory_space=pltpu.VMEM)
    smem = pl.BlockSpec(memory_space=pltpu.SMEM)
    entries = leaves * size * size * 8
    dma = pltpu.SemaphoreType.DMA
    out = pl.pallas_call(
        whole_kernel,
        in_specs=[vmem] * 6 + [smem] * 3,
        out_specs=vmem,
        out_shape=jax.ShapeDtypeStruct((columns, leaves * size), F32),
        scratch_shapes=[
            pltpu.VMEM((3 * leaves, width, size), F32),
            pltpu.VMEM((2 * ring, leaves + 1, width, skel), F32),
            pltpu.VMEM((leaves, DEPTH, size), BF16),
            pltpu.VMEM((leaves, 2 * columns, size), F32),
            dma((2,)), dma((2,)), dma((ring,)), dma((ring,)), dma((ring,)), dma((2 * ring,)),
        ],
        compiler_params=pltpu.CompilerParams(
            vmem_limit_bytes=56 * 1024 * 1024, collective_id=0, has_side_effects=True
        ),
        cost_estimate=pl.CostEstimate(
            flops=entries * 2 * 3 * 256, bytes_accessed=8 * 1024 * 1024, transcendentals=entries
        ),
        name="whole",
    )(
        points.T, rhs.T, leaf_interpolator, node_basis, leaf_skeleton, node_skeleton, near_list.T,
        far_owner[:, :, 0], far_node,
    )
    return out.T


def solution(mesh):
    rows = ("groups", "leaf", "sub")
    two, three = P(rows, None), P(rows, None, None)
    in_specs = (two, two, three, three, two, two, two, three, two)
    return jax.shard_map(
        per_device, mesh=mesh, in_specs=in_specs, out_specs=two, check_vma=False
    )
```
